512 devices in a mesh: grp: 32 (over z, core), mem: 16 (over y, x).
Axes of the slice: x: 4, y: 4, z: 16, core: 2. Of those that a mesh axis runs over, the one named last changes fastest.
Arguments:
- amplitudes: bfloat16 [4096, 16384], P('grp', 'mem'), may hold values from -6 to 6
- amp_tiles: int32 [32, 128], P('grp', 'mem'), may hold values 0 or 1
- integrals: bfloat16 [16384, 4096], P('mem', 'grp'), may hold values from -0.046875 to 0.046875
- int_tiles: int32 [128, 32], P('mem', 'grp'), may hold values from 0 to 1, as said below
- denominators: float32 [4096, 4096], P('grp', 'mem'), may hold values from 0.5 to 4
Outputs:
- update: bfloat16 [4096, 4096], P('grp', 'mem')
The draws below stay inside these ranges and needn't reach their ends.
Inputs may be any that keep to these rules, and one draw needn't show every extreme that they name: `int_tiles`: in each aligned block of 8 tile rows, every tile column holds exactly 6 ones.
All inputs are finite; a program needn't handle non-finite values. No bound on the sum of `amp_tiles` on one device may be relied on, other than what follows from the above.
Results may differ from the reference program's by a relative error of at most 0.001.
Values may be sent and summed in bfloat16 or wider, within the bound.
No kernel may reach another device: no remote copies, remote signals or barrier semaphores. Data moves between devices by JAX's collectives and lax.ppermute only.
A program may use at most 64 MiB of HBM per device.

```python
import math
import jax
import jax.numpy as jnp

TILE = 128
RT = 1
KT_DEV = 8
NZ = 6
ROWS = 4096
KT = 128
BTILES = 32
N_GRP = 32


def draw_int_tiles(key, part):
    key = jax.random.fold_in(key, 7)
    blocks = KT // KT_DEV
    keys = jax.random.split(key, blocks * BTILES)
    orders = jax.vmap(lambda k: jax.random.permutation(k, KT_DEV))(keys)
    chosen = (orders < NZ).astype(jnp.int32)
    chosen = chosen.reshape(blocks, BTILES, KT_DEV)
    return jnp.transpose(chosen, (0, 2, 1)).reshape(KT, BTILES)


def plant(drawn, stream_key, smallest, high):
    place = [jax.random.randint(jax.random.fold_in(stream_key, axis), (), 0, length) for axis, length in enumerate(drawn.shape)]
    main_axis = drawn.shape.index(max(drawn.shape))
    next_to = place[:main_axis] + [(place[main_axis] + 1) % drawn.shape[main_axis]] + place[main_axis + 1:]
    return drawn.at[tuple(place)].set(smallest).at[tuple(next_to)].set(high)


def block_levels(key, dims, pieces, least, top_value):
    factor_of = 1.0
    for axis_at, blocks in pieces:
        draws = jax.random.uniform(jax.random.fold_in(jax.random.fold_in(key, 6), axis_at), (blocks,), jnp.float32, least / len(pieces), top_value / len(pieces))
        factor_of = factor_of * jnp.repeat(jnp.exp(draws), dims[axis_at] // blocks).reshape((-1,) + (1,) * (len(dims) - 1 - axis_at))
    return factor_of


def normal_values(key, extent, spread, most, cuts=(), dtype=jnp.bfloat16):
    drawn = jax.random.normal(key, extent, jnp.float32) * spread
    if len(cuts) > 0:
        drawn = block_levels(key, extent, cuts, -0.22, 0.18) * drawn
    return jnp.clip(drawn, min=-most, max=most).astype(dtype)


def setup_inputs(seed: int = 0) -> dict:
    streams_of = jax.random.split(jax.random.key(seed), 6)
    return {
        "amplitudes": normal_values(streams_of[0], (ROWS, KT * TILE), 1.0, 6.0, ((0, 32), (1, 16))),
        "amp_tiles": plant((jax.random.randint(streams_of[1], (RT * N_GRP, KT), 0, 4) < 3).astype(jnp.int32), jax.random.fold_in(streams_of[1], 1), 0, 1),
        "integrals": normal_values(streams_of[2], (KT * TILE, BTILES * TILE), (KT * TILE) ** -0.5, 0.046875, ((0, 16), (1, 32))),
        "int_tiles": draw_int_tiles(jax.random.fold_in(streams_of[5], 71), 0),
        "denominators": jnp.clip(jnp.exp(math.log(4.0) - 2.0794415 * jax.random.uniform(streams_of[4], (ROWS, BTILES * TILE), jnp.float32) ** block_levels(streams_of[4], (ROWS, BTILES * TILE), ((0, 32), (1, 16)), -0.2, 0.2)), 0.5, 4.0),
    }


def expand(mask, tile):
    return jnp.repeat(jnp.repeat(mask, tile, axis=0), tile, axis=1)


def reference(amplitudes, amp_tiles, integrals, int_tiles, denominators):
    masked_amp = amplitudes * expand(amp_tiles, TILE).astype(jnp.bfloat16)
    masked_int = integrals * expand(int_tiles, TILE).astype(jnp.bfloat16)
    ladder = jnp.dot(masked_amp, masked_int, preferred_element_type=jnp.float32)
    return (ladder / denominators).astype(jnp.bfloat16)
```

```python
import jax
import jax.numpy as jnp
from jax import lax
from jax.sharding import PartitionSpec as P

NZ = 6
ROW = 16


def pick(options, which):
    out = options[-1]
    for at in range(len(options) - 2, -1, -1):
        out = jnp.where(which == at, options[at], out)
    return out


def pack(integrals, int_tiles, tile):
    kt = int_tiles.shape[0]
    blocks = integrals.reshape(kt, tile, tile)
    zeros = jnp.cumsum(1 - int_tiles[:, 0])
    slots = []
    for i in range(NZ):
        lag = sum((zeros[i + o] > o).astype(jnp.int32) for o in range(kt - NZ))
        slots.append(pick([blocks[i + o] for o in range(kt - NZ + 1)], lag))
    slots = jnp.stack(slots).astype(jnp.float32)
    top = jnp.max(jnp.abs(slots), axis=1)
    shift = jnp.clip(jnp.floor(14.0 - jnp.log2(jnp.maximum(top, 1e-37))), 0.0, 120.0)
    values = (slots * jnp.exp2(shift)[:, None, :]).astype(jnp.float16)
    mask = jnp.broadcast_to(int_tiles.astype(jnp.float32), (kt, tile))
    note = jnp.concatenate([shift, mask, jnp.zeros((ROW - NZ - kt, tile), jnp.float32)])
    return jnp.concatenate([values.reshape(NZ * tile, tile), note.astype(jnp.float16)])


def unpack(packed, kt, tile):
    groups = packed.shape[0]
    values = packed[:, : NZ * tile].reshape(groups, NZ, tile, tile).astype(jnp.float32)
    note = packed[:, NZ * tile :].astype(jnp.float32)
    shift, mask = note[:, :NZ], note[:, NZ : NZ + kt]
    slots = (values * jnp.exp2(-shift)[:, :, None, :]).astype(jnp.bfloat16)
    zeros = jnp.cumsum(1.0 - mask, axis=1)
    full = []
    for k in range(kt):
        out = jnp.zeros_like(slots[:, 0])
        for o in range(kt - NZ + 1):
            if 0 <= k - o < NZ:
                here = (mask[:, k] > 0) & (zeros[:, k] == o)
                out = jnp.where(here[:, None, :], slots[:, k - o], out)
        full.append(out)
    return jnp.concatenate(full, axis=1)


def on_device(amplitudes, amp_tiles, integrals, int_tiles, denominators):
    rows, depth = amplitudes.shape
    kt = int_tiles.shape[0]
    tile = depth // kt
    owners, width = lax.axis_size("mem"), denominators.shape[1]
    masked_amp = amplitudes * jnp.repeat(amp_tiles, tile, axis=1).astype(jnp.bfloat16)
    everyone = lax.all_gather(pack(integrals, int_tiles, tile), "grp")
    masked_int = unpack(everyone, kt, tile)
    masked_int = masked_int.reshape(owners, -1, depth, tile)
    partial_sum = jnp.einsum(
        "rk,obkc->orbc", masked_amp, masked_int, preferred_element_type=jnp.float32
    ).reshape(owners, rows, width)
    ladder = jnp.sum(lax.all_to_all(partial_sum, "mem", 0, 0), axis=0)
    return (ladder / denominators).astype(jnp.bfloat16)


def solution(mesh):
    return jax.shard_map(
        on_device,
        mesh=mesh,
        in_specs=(
            P("grp", "mem"),
            P("grp", "mem"),
            P("mem", "grp"),
            P("mem", "grp"),
            P("grp", "mem"),
        ),
        out_specs=P("grp", "mem"),
        check_vma=False,
    )
```

```python
import functools

import jax
import jax.numpy as jnp
from jax import lax
from jax.experimental import pallas as pl
from jax.experimental.pallas import tpu as pltpu
from jax.sharding import PartitionSpec as P

NZ = 6
NOTE = 16
FINE = 8.0
VMEM = pl.BlockSpec(memory_space=pltpu.VMEM)
SMEM = pl.BlockSpec(memory_space=pltpu.SMEM)


def to_int16(values):
    return jnp.round(values).astype(jnp.int32).astype(jnp.int16)


def note_of(rows, width):
    at = lax.broadcasted_iota(jnp.int32, (NOTE, width), 0)
    note = jnp.zeros((NOTE, width), jnp.float32)
    for i, row in enumerate(rows):
        note = jnp.where(at == i, row, note)
    return to_int16(note)


def pack_kernel(kt, tile, tiles_ref, integrals_ref, out_ref):
    ones = [tiles_ref[k, 0] for k in range(kt)]
    zeros = [sum(1 - ones[j] for j in range(k + 1)) for k in range(kt)]
    shifts = []
    for i in range(NZ):
        at = i
        for o in range(kt - NZ):
            at = at + (zeros[i + o] > o).astype(jnp.int32)
        start = pl.multiple_of(at * tile, tile)
        block = integrals_ref[pl.ds(start, tile), :].astype(jnp.float32)
        top = jnp.max(jnp.abs(block), axis=0, keepdims=True)
        shift = jnp.floor(14.99 - jnp.log2(jnp.maximum(top, 1e-37)))
        shift = jnp.clip(shift, 0.0, 120.0)
        out_ref[i * tile : (i + 1) * tile] = to_int16(block * jnp.exp2(shift))
        shifts.append(shift)
    mask = [one.astype(jnp.float32) for one in ones]
    out_ref[NZ * tile :] = note_of(shifts + mask, tile)


def ladder_kernel(kt, tile, tiles_ref, amp_ref, packed_ref, out_ref, masked, full):
    groups = out_ref.shape[0]
    per = packed_ref.shape[0] // groups
    rows = amp_ref.shape[0]

    @pl.when(pl.program_id(0) == 0)
    def _():
        for k in range(kt):
            cols = slice(k * tile, (k + 1) * tile)
            keep = tiles_ref[0, k].astype(jnp.float32)
            masked[:, cols] = (amp_ref[:, cols].astype(jnp.float32) * keep).astype(
                jnp.bfloat16
            )

    for g in range(groups):
        for j in range(per):
            b = g * per + j
            note = packed_ref[b, NZ * tile :].astype(jnp.int32).astype(jnp.float32)
            slots = []
            for i in range(NZ):
                block = packed_ref[b, i * tile : (i + 1) * tile]
                block = block.astype(jnp.int32).astype(jnp.float32)
                slots.append((block * jnp.exp2(-note[i : i + 1])).astype(jnp.bfloat16))
            zeros = jnp.zeros((1, tile), jnp.float32)
            for k in range(kt):
                one = note[NZ + k : NZ + k + 1]
                zeros = zeros + (1.0 - one)
                out = None
                for o in range(kt - NZ + 1):
                    if 0 <= k - o < NZ:
                        here = jnp.where(zeros == o, one, 0.0).astype(jnp.bfloat16)
                        term = slots[k - o] * here
                        out = term if out is None else out + term
                full[g, k * tile : (k + 1) * tile, j * tile : (j + 1) * tile] = out
        part = jnp.dot(masked[...], full[g], preferred_element_type=jnp.float32)
        top = jnp.max(jnp.abs(part), axis=0, keepdims=True)
        shift = jnp.floor(FINE * (14.999 - jnp.log2(jnp.maximum(top, 1e-30))))
        out_ref[g, :rows] = to_int16(part * jnp.exp2(shift / FINE))
        out_ref[g, rows:] = note_of([shift], part.shape[1])


def update_kernel(parts_ref, denominators_ref, out_ref):
    rows = denominators_ref.shape[0]
    total = jnp.zeros(denominators_ref.shape, jnp.float32)
    for i in range(parts_ref.shape[0]):
        note = parts_ref[i, rows:].astype(jnp.int32).astype(jnp.float32)
        part = parts_ref[i, :rows].astype(jnp.int32).astype(jnp.float32)
        total = total + part * jnp.exp2(note[:1] / -FINE)
    out_ref[...] = (total / denominators_ref[...]).astype(out_ref.dtype)


def on_device(amplitudes, amp_tiles, integrals, int_tiles, denominators):
    rows, depth = amplitudes.shape
    kt = int_tiles.shape[0]
    tile = depth // kt
    owners, width = lax.axis_size("mem"), denominators.shape[1]
    packed = pl.pallas_call(
        functools.partial(pack_kernel, kt, tile),
        out_shape=jax.ShapeDtypeStruct((NZ * tile + NOTE, tile), jnp.int16),
        in_specs=[SMEM, VMEM],
        out_specs=VMEM,
        name="pack",
    )(int_tiles, integrals)
    everyone = lax.all_gather(packed, "grp")
    per = width // tile
    step = 2
    parts = pl.pallas_call(
        functools.partial(ladder_kernel, kt, tile),
        out_shape=jax.ShapeDtypeStruct((owners, rows + NOTE, width), jnp.int16),
        grid=(owners // step,),
        in_specs=[
            SMEM,
            pl.BlockSpec((rows, depth), lambda s: (0, 0)),
            pl.BlockSpec((step * per, NZ * tile + NOTE, tile), lambda s: (s, 0, 0)),
        ],
        out_specs=pl.BlockSpec((step, rows + NOTE, width), lambda s: (s, 0, 0)),
        scratch_shapes=[
            pltpu.VMEM((rows, depth), jnp.bfloat16),
            pltpu.VMEM((step, depth, width), jnp.bfloat16),
        ],
        compiler_params=pltpu.CompilerParams(vmem_limit_bytes=32 * 2**20),
        name="ladder",
    )(amp_tiles, amplitudes, everyone)
    return pl.pallas_call(
        update_kernel,
        out_shape=jax.ShapeDtypeStruct((rows, width), jnp.bfloat16),
        in_specs=[VMEM, VMEM],
        out_specs=VMEM,
        name="update",
    )(lax.all_to_all(parts, "mem", 0, 0), denominators)


def solution(mesh):
    return jax.shard_map(
        on_device,
        mesh=mesh,
        in_specs=(
            P("grp", "mem"),
            P("grp", "mem"),
            P("mem", "grp"),
            P("mem", "grp"),
            P("grp", "mem"),
        ),
        out_specs=P("grp", "mem"),
        check_vma=False,
    )
```

```python
import functools

import jax
import jax.numpy as jnp
from jax import lax
from jax.experimental import pallas as pl
from jax.experimental.pallas import tpu as pltpu
from jax.sharding import PartitionSpec as P

NZ = 6
NOTE = 16
LAG = 256.0
FINE = 8.0
VMEM = pl.BlockSpec(memory_space=pltpu.VMEM)
SMEM = pl.BlockSpec(memory_space=pltpu.SMEM)


def to_int16(values):
    return jnp.round(values).astype(jnp.int32).astype(jnp.int16)


def note_of(rows, width):
    at = lax.broadcasted_iota(jnp.int32, (NOTE, width), 0)
    note = jnp.zeros((NOTE, width), jnp.float32)
    for i, row in enumerate(rows):
        note = jnp.where(at == i, row, note)
    return to_int16(note)


def pack_kernel(kt, tile, tiles_ref, integrals_ref, out_ref):
    ones = [tiles_ref[0, k] for k in range(kt)]
    zeros = [sum(1 - ones[j] for j in range(k + 1)) for k in range(kt)]
    notes = []
    for i in range(NZ):
        lag = 0
        for o in range(kt - NZ):
            lag = lag + (zeros[i + o] > o).astype(jnp.int32)
        start = pl.multiple_of((i + lag) * tile, tile)
        block = integrals_ref[pl.ds(start, tile), :].astype(jnp.float32)
        top = jnp.max(jnp.abs(block), axis=0, keepdims=True)
        shift = jnp.floor(14.99 - jnp.log2(jnp.maximum(top, 1e-37)))
        shift = jnp.clip(shift, 0.0, 120.0)
        out_ref[i * tile : (i + 1) * tile] = to_int16(block * jnp.exp2(shift))
        notes.append(shift + LAG * lag.astype(jnp.float32))
    out_ref[NZ * tile :] = note_of(notes, tile)


def ladder_kernel(kt, tile, tiles_ref, amp_ref, packed_ref, out_ref, masked, full):
    groups = out_ref.shape[0]
    per = packed_ref.shape[0] // groups
    rows = amp_ref.shape[0]

    @pl.when(pl.program_id(0) == 0)
    def _():
        for k in range(kt):
            cols = slice(k * tile, (k + 1) * tile)
            keep = tiles_ref[0, k].astype(jnp.float32)
            masked[:, cols] = (amp_ref[:, cols].astype(jnp.float32) * keep).astype(
                jnp.bfloat16
            )

    for g in range(groups):
        for j in range(per):
            b = g * per + j
            note = packed_ref[b, NZ * tile :].astype(jnp.int32).astype(jnp.float32)
            lag = jnp.floor(note / LAG)
            scale = jnp.exp2(LAG * lag - note)
            lags = range(kt - NZ + 1)
            place = [jnp.where(lag == o, scale, 0.0).astype(jnp.bfloat16) for o in lags]
            slots = []
            for i in range(NZ):
                block = packed_ref[b, i * tile : (i + 1) * tile].astype(jnp.int32)
                slots.append(block.astype(jnp.float32).astype(jnp.bfloat16))
            for k in range(kt):
                out = None
                for o in lags:
                    i = k - o
                    if 0 <= i < NZ:
                        term = slots[i] * place[o][i : i + 1]
                        out = term if out is None else out + term
                full[g, k * tile : (k + 1) * tile, j * tile : (j + 1) * tile] = out
        part = jnp.dot(masked[...], full[g], preferred_element_type=jnp.float32)
        top = jnp.max(jnp.abs(part), axis=0, keepdims=True)
        shift = jnp.floor(FINE * (14.999 - jnp.log2(jnp.maximum(top, 1e-30))))
        out_ref[g, :rows] = to_int16(part * jnp.exp2(shift / FINE))
        out_ref[g, rows:] = note_of([shift], part.shape[1])


def update_kernel(parts_ref, denominators_ref, out_ref):
    rows = denominators_ref.shape[0]
    total = jnp.zeros(denominators_ref.shape, jnp.float32)
    for i in range(parts_ref.shape[0]):
        note = parts_ref[i, rows:].astype(jnp.int32).astype(jnp.float32)
        part = parts_ref[i, :rows].astype(jnp.int32).astype(jnp.float32)
        total = total + part * jnp.exp2(note[:1] / -FINE)
    out_ref[...] = (total / denominators_ref[...]).astype(out_ref.dtype)


def on_device(amplitudes, amp_tiles, integrals, int_tiles, denominators):
    rows, depth = amplitudes.shape
    kt = int_tiles.shape[0]
    tile = depth // kt
    owners, width = lax.axis_size("mem"), denominators.shape[1]
    packed = pl.pallas_call(
        functools.partial(pack_kernel, kt, tile),
        out_shape=jax.ShapeDtypeStruct((NZ * tile + NOTE, tile), jnp.int16),
        in_specs=[SMEM, VMEM],
        out_specs=VMEM,
        name="pack",
    )(int_tiles.reshape(1, kt), integrals)
    everyone = lax.all_gather(packed, "grp")
    per = width // tile
    step = 4
    parts = pl.pallas_call(
        functools.partial(ladder_kernel, kt, tile),
        out_shape=jax.ShapeDtypeStruct((owners, rows + NOTE, width), jnp.int16),
        grid=(owners // step,),
        in_specs=[
            SMEM,
            pl.BlockSpec((rows, depth), lambda s: (0, 0)),
            pl.BlockSpec((step * per, NZ * tile + NOTE, tile), lambda s: (s, 0, 0)),
        ],
        out_specs=pl.BlockSpec((step, rows + NOTE, width), lambda s: (s, 0, 0)),
        scratch_shapes=[
            pltpu.VMEM((rows, depth), jnp.bfloat16),
            pltpu.VMEM((step, depth, width), jnp.bfloat16),
        ],
        compiler_params=pltpu.CompilerParams(vmem_limit_bytes=32 * 2**20),
        name="ladder",
    )(amp_tiles, amplitudes, everyone)
    return pl.pallas_call(
        update_kernel,
        out_shape=jax.ShapeDtypeStruct((rows, width), jnp.bfloat16),
        in_specs=[VMEM, VMEM],
        out_specs=VMEM,
        name="update",
    )(lax.all_to_all(parts, "mem", 0, 0), denominators)


def solution(mesh):
    return jax.shard_map(
        on_device,
        mesh=mesh,
        in_specs=(
            P("grp", "mem"),
            P("grp", "mem"),
            P("mem", "grp"),
            P("mem", "grp"),
            P("grp", "mem"),
        ),
        out_specs=P("grp", "mem"),
        check_vma=False,
    )
```

```python
import functools

import jax
import jax.numpy as jnp
from jax import lax
from jax.experimental import pallas as pl
from jax.experimental.pallas import tpu as pltpu
from jax.sharding import PartitionSpec as P

NZ = 6
NOTE = 16
FINE = 8.0
VMEM = pl.BlockSpec(memory_space=pltpu.VMEM)
SMEM = pl.BlockSpec(memory_space=pltpu.SMEM)


def to_int16(values):
    return jnp.round(values).astype(jnp.int32).astype(jnp.int16)


def note_of(rows, width):
    at = lax.broadcasted_iota(jnp.int32, (NOTE, width), 0)
    note = jnp.zeros((NOTE, width), jnp.float32)
    for i, row in enumerate(rows):
        note = jnp.where(at == i, row, note)
    return note


def pack_kernel(kt, tile, int_ref, amp_tiles_ref, integrals_ref, amp_ref, out_ref, masked_ref):
    ones = [int_ref[0, k] for k in range(kt)]
    zeros = [sum(1 - ones[j] for j in range(k + 1)) for k in range(kt)]
    lags = []
    for i in range(NZ):
        lag = 0
        for o in range(kt - NZ):
            lag = lag + (zeros[i + o] > o).astype(jnp.int32)
        start = pl.multiple_of((i + lag) * tile, tile)
        out_ref[i * tile : (i + 1) * tile] = integrals_ref[pl.ds(start, tile), :]
        lags.append(lag.astype(jnp.float32))
    out_ref[NZ * tile :] = note_of(lags, tile).astype(jnp.bfloat16)
    for k in range(kt):
        cols = slice(k * tile, (k + 1) * tile)
        keep = amp_tiles_ref[0, k].astype(jnp.float32)
        masked_ref[:, cols] = (amp_ref[:, cols].astype(jnp.float32) * keep).astype(
            jnp.bfloat16
        )


def ladder_kernel(kt, tile, amp_ref, left_ref, right_ref, *rest):
    out_ref, full = rest[-2:]
    pieces, height, width = out_ref.shape
    rows = height - NOTE
    lags = range(kt - NZ + 1)
    for j, block_ref in enumerate((left_ref, right_ref)):
        note = block_ref[NZ * tile :].astype(jnp.float32)
        place = [jnp.where(note == o, 1.0, 0.0).astype(jnp.bfloat16) for o in lags]
        slots = [block_ref[i * tile : (i + 1) * tile] for i in range(NZ)]
        for k in range(kt):
            out = None
            for o in lags:
                i = k - o
                if 0 <= i < NZ:
                    term = slots[i] * place[o][i : i + 1]
                    out = term if out is None else out + term
            full[k * tile : (k + 1) * tile, j * tile : (j + 1) * tile] = out
    sums = jnp.dot(amp_ref[...], full[...], preferred_element_type=jnp.float32)
    for p in range(pieces):
        part = sums[p * rows : (p + 1) * rows]
        top = jnp.max(jnp.abs(part), axis=0, keepdims=True)
        shift = jnp.floor(FINE * (14.999 - jnp.log2(jnp.maximum(top, 1e-30))))
        out_ref[p, :rows] = to_int16(part * jnp.exp2(shift / FINE))
        out_ref[p, rows:] = to_int16(note_of([shift], width))


def sum_kernel(core_ref, parts_ref, first_ref, second_ref):
    rows, half = first_ref.shape
    total = jnp.zeros((rows, 2 * half), jnp.float32)
    for i in range(parts_ref.shape[0]):
        note = parts_ref[i, rows:].astype(jnp.int32).astype(jnp.float32)
        part = parts_ref[i, :rows].astype(jnp.int32).astype(jnp.float32)
        total = total + part * jnp.exp2(note[:1] / -FINE)
    left, right = total[:, :half], total[:, half:]
    swap = core_ref[0, 0] == 1
    first_ref[...] = jnp.where(swap, right, left)
    second_ref[...] = jnp.where(swap, left, right)


def update_kernel(swap_ref, first_ref, second_ref, denominators_ref, out_ref):
    half = first_ref.shape[1]
    swap = swap_ref[0, 0] == 1
    first, second = first_ref[...], second_ref[...]
    left = jnp.where(swap, second, first) / denominators_ref[:, :half]
    right = jnp.where(swap, first, second) / denominators_ref[:, half:]
    out_ref[:, :half] = left.astype(out_ref.dtype)
    out_ref[:, half:] = right.astype(out_ref.dtype)


def routes(planes, owners):
    first, second = [], []
    for z in range(planes):
        for c in range(2):
            for m in range(owners):
                step, row = divmod(m, 4)
                if step < 3:
                    to = [(z + (2 * c - 1) * 2 * (step + 1)) % planes] * 2
                else:
                    to = [z, (z + planes // 2) % planes][:: 1 - 2 * c]
                grp = 2 * (z ^ (row // 2)) + (c ^ (row % 2))
                me = (2 * z + c) * owners + m
                first.append((me, grp * owners + to[0]))
                second.append((me, grp * owners + to[1]))
    return first, second


def on_device(amplitudes, amp_tiles, integrals, int_tiles, denominators):
    rows, depth = amplitudes.shape
    kt = int_tiles.shape[0]
    tile = depth // kt
    groups, owners = lax.axis_size("grp"), lax.axis_size("mem")
    planes, width = groups // 2, denominators.shape[1]
    grp, mem = lax.axis_index("grp"), lax.axis_index("mem")
    plane, core = grp // 2, grp % 2

    other_core = [(g, g ^ 1) for g in range(groups)]
    other_plane = [(g, g ^ 2) for g in range(groups)]
    onward = [(g, (g + (4 if g % 2 == 0 else -4)) % groups) for g in range(groups)]

    own, masked = pl.pallas_call(
        functools.partial(pack_kernel, kt, tile),
        out_shape=(
            jax.ShapeDtypeStruct((NZ * tile + NOTE, tile), jnp.bfloat16),
            jax.ShapeDtypeStruct((rows, depth), jnp.bfloat16),
        ),
        in_specs=[SMEM, SMEM, VMEM, VMEM],
        out_specs=(VMEM, VMEM),
        name="pack",
    )(int_tiles.reshape(1, kt), amp_tiles, integrals, amplitudes)
    partner = lax.ppermute(own, "grp", other_core)
    lefts, rights = [own], [partner]
    for s in range(4):
        lefts.append(lax.ppermute(lefts[-1], "grp", onward))
        if s < 3:
            rights.append(lax.ppermute(rights[-1], "grp", onward))

    beside = lax.ppermute(masked, "grp", other_core)
    across = lax.ppermute(masked, "grp", other_plane)
    amps = jnp.concatenate(
        [masked, beside, across, lax.ppermute(across, "grp", other_core)], axis=0
    )

    parts = None
    for s in range(4):
        pair = (lefts[s + 1], rights[s + 1]) if s < 3 else (own, lefts[4])
        parts = pl.pallas_call(
            functools.partial(ladder_kernel, kt, tile),
            out_shape=jax.ShapeDtypeStruct((owners, rows + NOTE, width), jnp.int16),
            grid=(1,),
            in_specs=[
                pl.BlockSpec((4 * rows, depth), lambda i: (0, 0)),
                pl.BlockSpec((NZ * tile + NOTE, tile), lambda i: (0, 0)),
                pl.BlockSpec((NZ * tile + NOTE, tile), lambda i: (0, 0)),
            ]
            + ([] if parts is None else [pl.BlockSpec(memory_space=pl.ANY)]),
            out_specs=pl.BlockSpec(
                (4, rows + NOTE, width), functools.partial(lambda s, i: (s, 0, 0), s)
            ),
            scratch_shapes=[pltpu.VMEM((depth, width), jnp.bfloat16)],
            input_output_aliases={} if parts is None else {3: 0},
            cost_estimate=pl.CostEstimate(
                flops=8 * rows * depth * width, bytes_accessed=2**21, transcendentals=0
            ),
            compiler_params=pltpu.CompilerParams(vmem_limit_bytes=32 * 2**20),
            name="ladder",
        )(amps, *pair, *([] if parts is None else [parts]))

    half = jax.ShapeDtypeStruct((rows, tile), jnp.float32)
    first, second = pl.pallas_call(
        sum_kernel,
        out_shape=(half, half),
        in_specs=[SMEM, VMEM],
        out_specs=(VMEM, VMEM),
        name="sum",
    )(core.reshape(1, 1), lax.all_to_all(parts, "mem", 0, 0))
    to_first, to_second = routes(planes, owners)
    first = lax.ppermute(first, ("grp", "mem"), to_first)
    second = lax.ppermute(second, ("grp", "mem"), to_second)
    source = jnp.bitwise_xor(plane, jnp.bitwise_and(plane + mem, 1))
    swap = (mem == (source + planes // 2) % planes).astype(jnp.int32)
    return pl.pallas_call(
        update_kernel,
        out_shape=jax.ShapeDtypeStruct((rows, width), jnp.bfloat16),
        in_specs=[SMEM, VMEM, VMEM, VMEM],
        out_specs=VMEM,
        name="update",
    )(swap.reshape(1, 1), first, second, denominators)


def solution(mesh):
    return jax.shard_map(
        on_device,
        mesh=mesh,
        in_specs=(
            P("grp", "mem"),
            P("grp", "mem"),
            P("mem", "grp"),
            P("mem", "grp"),
            P("grp", "mem"),
        ),
        out_specs=P("grp", "mem"),
        check_vma=False,
    )
```

```python
import functools

import jax
import jax.numpy as jnp
from jax import lax
from jax.experimental import pallas as pl
from jax.experimental.pallas import tpu as pltpu
from jax.sharding import PartitionSpec as P

NZ = 6
NOTE = 16
LAG = 256.0
FINE = 8.0
VMEM = pl.BlockSpec(memory_space=pltpu.VMEM)
SMEM = pl.BlockSpec(memory_space=pltpu.SMEM)


def to_int16(values):
    return jnp.round(values).astype(jnp.int32).astype(jnp.int16)


def note_of(rows, width):
    at = lax.broadcasted_iota(jnp.int32, (NOTE, width), 0)
    note = jnp.zeros((NOTE, width), jnp.float32)
    for i, row in enumerate(rows):
        note = jnp.where(at == i, row, note)
    return to_int16(note)


def pack_kernel(kt, tile, tiles_ref, integrals_ref, out_ref):
    ones = [tiles_ref[0, k] for k in range(kt)]
    zeros = [sum(1 - ones[j] for j in range(k + 1)) for k in range(kt)]
    notes = []
    for i in range(NZ):
        lag = 0
        for o in range(kt - NZ):
            lag = lag + (zeros[i + o] > o).astype(jnp.int32)
        start = pl.multiple_of((i + lag) * tile, tile)
        block = integrals_ref[pl.ds(start, tile), :].astype(jnp.float32)
        top = jnp.max(jnp.abs(block), axis=0, keepdims=True)
        shift = jnp.floor(14.99 - jnp.log2(jnp.maximum(top, 1e-37)))
        shift = jnp.clip(shift, 0.0, 120.0)
        out_ref[i * tile : (i + 1) * tile] = to_int16(block * jnp.exp2(shift))
        notes.append(shift + LAG * lag.astype(jnp.float32))
    out_ref[NZ * tile :] = note_of(notes, tile)


def ladder_kernel(kt, tile, tiles_ref, amp_ref, packed_ref, out_ref, masked, full):
    groups = out_ref.shape[0]
    per = packed_ref.shape[0] // groups
    rows = amp_ref.shape[0]

    @pl.when(pl.program_id(0) == 0)
    def _():
        for k in range(kt):
            cols = slice(k * tile, (k + 1) * tile)
            keep = tiles_ref[0, k].astype(jnp.float32)
            masked[:, cols] = (amp_ref[:, cols].astype(jnp.float32) * keep).astype(
                jnp.bfloat16
            )

    for g in range(groups):
        for j in range(per):
            b = g * per + j
            note = packed_ref[b, NZ * tile :].astype(jnp.int32).astype(jnp.float32)
            lag = jnp.floor(note / LAG)
            scale = jnp.exp2(LAG * lag - note)
            lags = range(kt - NZ + 1)
            place = [jnp.where(lag == o, scale, 0.0).astype(jnp.bfloat16) for o in lags]
            slots = []
            for i in range(NZ):
                block = packed_ref[b, i * tile : (i + 1) * tile].astype(jnp.int32)
                slots.append(block.astype(jnp.float32).astype(jnp.bfloat16))
            for k in range(kt):
                out = None
                for o in lags:
                    i = k - o
                    if 0 <= i < NZ:
                        term = slots[i] * place[o][i : i + 1]
                        out = term if out is None else out + term
                full[g % full.shape[0], k * tile : (k + 1) * tile, j * tile : (j + 1) * tile] = out
        part = jnp.dot(masked[...], full[g % full.shape[0]], preferred_element_type=jnp.float32)
        top = jnp.max(jnp.abs(part), axis=0, keepdims=True)
        shift = jnp.floor(FINE * (14.999 - jnp.log2(jnp.maximum(top, 1e-30))))
        out_ref[g, :rows] = to_int16(part * jnp.exp2(shift / FINE))
        out_ref[g, rows:] = note_of([shift], part.shape[1])


def on_device(amplitudes, amp_tiles, integrals, int_tiles, denominators):
    rows, depth = amplitudes.shape
    kt = int_tiles.shape[0]
    tile = depth // kt
    owners, width = lax.axis_size("mem"), denominators.shape[1]
    packed = pl.pallas_call(
        functools.partial(pack_kernel, kt, tile),
        out_shape=jax.ShapeDtypeStruct((NZ * tile + NOTE, tile), jnp.int16),
        in_specs=[SMEM, VMEM],
        out_specs=VMEM,
        name="pack",
    )(int_tiles.reshape(1, kt), integrals)
    everyone = lax.all_gather(packed, "grp")
    per = width // tile
    step = 16
    parts = pl.pallas_call(
        functools.partial(ladder_kernel, kt, tile),
        out_shape=jax.ShapeDtypeStruct((owners, rows + NOTE, width), jnp.int16),
        grid=(owners // step,),
        in_specs=[
            SMEM,
            pl.BlockSpec((rows, depth), lambda s: (0, 0)),
            pl.BlockSpec((step * per, NZ * tile + NOTE, tile), lambda s: (s, 0, 0)),
        ],
        out_specs=pl.BlockSpec((step, rows + NOTE, width), lambda s: (s, 0, 0)),
        scratch_shapes=[
            pltpu.VMEM((rows, depth), jnp.bfloat16),
            pltpu.VMEM((2, depth, width), jnp.bfloat16),
        ],
        compiler_params=pltpu.CompilerParams(vmem_limit_bytes=20 * 2**20),
        name="ladder",
    )(amp_tiles, amplitudes, everyone)
    parts = lax.all_to_all(parts, "mem", 0, 0)
    scale = jnp.exp2(parts[:, rows : rows + 1].astype(jnp.float32) / -FINE)
    ladder = jnp.sum(parts[:, :rows].astype(jnp.float32) * scale, axis=0)
    return (ladder / denominators).astype(jnp.bfloat16)


def solution(mesh):
    return jax.shard_map(
        on_device,
        mesh=mesh,
        in_specs=(
            P("grp", "mem"),
            P("grp", "mem"),
            P("mem", "grp"),
            P("mem", "grp"),
            P("grp", "mem"),
        ),
        out_specs=P("grp", "mem"),
        check_vma=False,
    )
```

```python
import functools

import jax
import jax.numpy as jnp
from jax import lax
from jax.experimental import pallas as pl
from jax.experimental.pallas import tpu as pltpu
from jax.sharding import PartitionSpec as P

NZ = 6
NOTE = 16
LAG = 256.0
FINE = 8.0
VMEM = pl.BlockSpec(memory_space=pltpu.VMEM)
SMEM = pl.BlockSpec(memory_space=pltpu.SMEM)


def to_int16(values):
    return jnp.round(values).astype(jnp.int32).astype(jnp.int16)


def note_of(rows, width):
    at = lax.broadcasted_iota(jnp.int32, (NOTE, width), 0)
    note = jnp.zeros((NOTE, width), jnp.float32)
    for i, row in enumerate(rows):
        note = jnp.where(at == i, row, note)
    return to_int16(note)


def pack_kernel(kt, tile, tiles_ref, integrals_ref, out_ref):
    ones = [tiles_ref[0, k] for k in range(kt)]
    zeros = [sum(1 - ones[j] for j in range(k + 1)) for k in range(kt)]
    notes = []
    for i in range(NZ):
        lag = 0
        for o in range(kt - NZ):
            lag = lag + (zeros[i + o] > o).astype(jnp.int32)
        start = pl.multiple_of((i + lag) * tile, tile)
        block = integrals_ref[pl.ds(start, tile), :].astype(jnp.float32)
        top = jnp.max(jnp.abs(block), axis=0, keepdims=True)
        shift = jnp.floor(14.99 - jnp.log2(jnp.maximum(top, 1e-37)))
        shift = jnp.clip(shift, 0.0, 120.0)
        out_ref[i * tile : (i + 1) * tile] = to_int16(block * jnp.exp2(shift))
        notes.append(shift + LAG * lag.astype(jnp.float32))
    out_ref[NZ * tile :] = note_of(notes, tile)


def ladder_kernel(kt, tile, tiles_ref, amp_ref, packed_ref, out_ref, masked):
    groups = out_ref.shape[0]
    per = packed_ref.shape[0] // groups
    rows = amp_ref.shape[0]

    @pl.when(pl.program_id(0) == 0)
    def _():
        for k in range(kt):
            cols = slice(k * tile, (k + 1) * tile)
            keep = tiles_ref[0, k].astype(jnp.float32)
            masked[:, cols] = (amp_ref[:, cols].astype(jnp.float32) * keep).astype(
                jnp.bfloat16
            )

    for g in range(groups):
        full = []
        for j in range(per):
            b = g * per + j
            note = packed_ref[b, NZ * tile :].astype(jnp.int32).astype(jnp.float32)
            lag = jnp.floor(note / LAG)
            scale = jnp.exp2(LAG * lag - note)
            lags = range(kt - NZ + 1)
            place = [jnp.where(lag == o, scale, 0.0).astype(jnp.bfloat16) for o in lags]
            slots = []
            for i in range(NZ):
                block = packed_ref[b, i * tile : (i + 1) * tile]
                slots.append(block.astype(jnp.bfloat16))
            tiles = []
            for k in range(kt):
                out = None
                for o in lags:
                    i = k - o
                    if 0 <= i < NZ:
                        term = slots[i] * place[o][i : i + 1]
                        out = term if out is None else out + term
                tiles.append(out)
            full.append(tiles)
        part = None
        for k in range(0, kt, 2):
            chunk = jnp.concatenate(
                [jnp.concatenate([t[k], t[k + 1]], axis=0) for t in full], axis=1
            )
            term = jnp.dot(
                masked[:, k * tile : (k + 2) * tile],
                chunk,
                preferred_element_type=jnp.float32,
            )
            part = term if part is None else part + term
        top = jnp.max(jnp.abs(part), axis=0, keepdims=True)
        shift = jnp.floor(FINE * (14.999 - jnp.log2(jnp.maximum(top, 1e-30))))
        out_ref[g, :rows] = to_int16(part * jnp.exp2(shift / FINE))
        out_ref[g, rows:] = note_of([shift], part.shape[1])


def on_device(amplitudes, amp_tiles, integrals, int_tiles, denominators):
    rows, depth = amplitudes.shape
    kt = int_tiles.shape[0]
    tile = depth // kt
    owners, width = lax.axis_size("mem"), denominators.shape[1]
    packed = pl.pallas_call(
        functools.partial(pack_kernel, kt, tile),
        out_shape=jax.ShapeDtypeStruct((NZ * tile + NOTE, tile), jnp.int16),
        in_specs=[SMEM, VMEM],
        out_specs=VMEM,
        name="pack",
    )(int_tiles.reshape(1, kt), integrals)
    everyone = lax.all_gather(packed, "grp")
    per = width // tile
    step = 16
    parts = pl.pallas_call(
        functools.partial(ladder_kernel, kt, tile),
        out_shape=jax.ShapeDtypeStruct((owners, rows + NOTE, width), jnp.int16),
        grid=(owners // step,),
        in_specs=[
            SMEM,
            pl.BlockSpec((rows, depth), lambda s: (0, 0)),
            pl.BlockSpec((step * per, NZ * tile + NOTE, tile), lambda s: (s, 0, 0)),
        ],
        out_specs=pl.BlockSpec((step, rows + NOTE, width), lambda s: (s, 0, 0)),
        scratch_shapes=[
            pltpu.VMEM((rows, depth), jnp.bfloat16),
        ],
        compiler_params=pltpu.CompilerParams(vmem_limit_bytes=20 * 2**20),
        name="ladder",
    )(amp_tiles, amplitudes, everyone)
    parts = lax.all_to_all(parts, "mem", 0, 0)
    scale = jnp.exp2(parts[:, rows : rows + 1].astype(jnp.float32) / -FINE)
    ladder = jnp.sum(parts[:, :rows].astype(jnp.float32) * scale, axis=0)
    return (ladder / denominators).astype(jnp.bfloat16)


def solution(mesh):
    return jax.shard_map(
        on_device,
        mesh=mesh,
        in_specs=(
            P("grp", "mem"),
            P("grp", "mem"),
            P("mem", "grp"),
            P("mem", "grp"),
            P("grp", "mem"),
        ),
        out_specs=P("grp", "mem"),
        check_vma=False,
    )
```

```python
import functools

import jax
import jax.numpy as jnp
from jax import lax
from jax.experimental import pallas as pl
from jax.experimental.pallas import tpu as pltpu
from jax.sharding import PartitionSpec as P

NZ = 6
NOTE = 8
LAG = 256.0
FINE = 8.0
VMEM = pl.BlockSpec(memory_space=pltpu.VMEM)
SMEM = pl.BlockSpec(memory_space=pltpu.SMEM)


def to_int16(values):
    return jnp.round(values).astype(jnp.int32).astype(jnp.int16)


def note_of(rows, width):
    at = lax.broadcasted_iota(jnp.int32, (NOTE, width), 0)
    note = jnp.zeros((NOTE, width), jnp.float32)
    for i, row in enumerate(rows):
        note = jnp.where(at == i, row, note)
    return to_int16(note)


def pack_kernel(kt, tile, tiles_ref, integrals_ref, out_ref):
    ones = [tiles_ref[0, k] for k in range(kt)]
    zeros = [sum(1 - ones[j] for j in range(k + 1)) for k in range(kt)]
    notes = []
    for i in range(NZ):
        lag = 0
        for o in range(kt - NZ):
            lag = lag + (zeros[i + o] > o).astype(jnp.int32)
        start = pl.multiple_of((i + lag) * tile, tile)
        block = integrals_ref[pl.ds(start, tile), :].astype(jnp.float32)
        top = jnp.max(jnp.abs(block), axis=0, keepdims=True)
        shift = jnp.floor(14.99 - jnp.log2(jnp.maximum(top, 1e-37)))
        shift = jnp.clip(shift, 0.0, 120.0)
        out_ref[i * tile : (i + 1) * tile] = to_int16(block * jnp.exp2(shift))
        notes.append(shift + LAG * lag.astype(jnp.float32))
    out_ref[NZ * tile :] = note_of(notes, tile)


def ladder_kernel(kt, tile, tiles_ref, amp_ref, packed_ref, out_ref, masked):
    groups = out_ref.shape[0]
    per = packed_ref.shape[0] // groups
    rows = amp_ref.shape[0]

    @pl.when(pl.program_id(0) == 0)
    def _():
        for k in range(kt):
            cols = slice(k * tile, (k + 1) * tile)
            keep = tiles_ref[0, k].astype(jnp.float32)
            masked[:, cols] = (amp_ref[:, cols].astype(jnp.float32) * keep).astype(
                jnp.bfloat16
            )

    for g in range(groups):
        full = []
        for j in range(per):
            b = g * per + j
            note = packed_ref[b, NZ * tile :].astype(jnp.int32).astype(jnp.float32)
            lag = jnp.floor(note / LAG)
            scale = jnp.exp2(LAG * lag - note)
            lags = range(kt - NZ + 1)
            place = [jnp.where(lag == o, scale, 0.0).astype(jnp.bfloat16) for o in lags]
            slots = []
            for i in range(NZ):
                block = packed_ref[b, i * tile : (i + 1) * tile]
                slots.append(block.astype(jnp.bfloat16))
            tiles = []
            for k in range(kt):
                out = None
                for o in lags:
                    i = k - o
                    if 0 <= i < NZ:
                        term = slots[i] * place[o][i : i + 1]
                        out = term if out is None else out + term
                tiles.append(out)
            full.append(tiles)
        part = None
        for k in range(0, kt, 2):
            chunk = jnp.concatenate(
                [jnp.concatenate([t[k], t[k + 1]], axis=0) for t in full], axis=1
            )
            term = jnp.dot(
                masked[:, k * tile : (k + 2) * tile],
                chunk,
                preferred_element_type=jnp.float32,
            )
            part = term if part is None else part + term
        top = jnp.max(jnp.abs(part), axis=0, keepdims=True)
        shift = jnp.floor(FINE * (14.999 - jnp.log2(jnp.maximum(top, 1e-37))))
        shift = jnp.minimum(shift, FINE * 125.0)
        out_ref[g, :rows] = to_int16(part * jnp.exp2(shift / FINE))
        out_ref[g, rows:] = note_of([shift], part.shape[1])


def on_device(amplitudes, amp_tiles, integrals, int_tiles, denominators):
    rows, depth = amplitudes.shape
    kt = int_tiles.shape[0]
    tile = depth // kt
    owners, width = lax.axis_size("mem"), denominators.shape[1]
    packed = pl.pallas_call(
        functools.partial(pack_kernel, kt, tile),
        out_shape=jax.ShapeDtypeStruct((NZ * tile + NOTE, tile), jnp.int16),
        in_specs=[SMEM, VMEM],
        out_specs=VMEM,
        name="pack",
    )(int_tiles.reshape(1, kt), integrals)
    everyone = lax.all_gather(packed, "grp")
    per = width // tile
    step = 16
    parts = pl.pallas_call(
        functools.partial(ladder_kernel, kt, tile),
        out_shape=jax.ShapeDtypeStruct((owners, rows + NOTE, width), jnp.int16),
        grid=(owners // step,),
        in_specs=[
            SMEM,
            pl.BlockSpec((rows, depth), lambda s: (0, 0)),
            pl.BlockSpec((step * per, NZ * tile + NOTE, tile), lambda s: (s, 0, 0)),
        ],
        out_specs=pl.BlockSpec((step, rows + NOTE, width), lambda s: (s, 0, 0)),
        scratch_shapes=[
            pltpu.VMEM((rows, depth), jnp.bfloat16),
        ],
        compiler_params=pltpu.CompilerParams(vmem_limit_bytes=20 * 2**20),
        name="ladder",
    )(amp_tiles, amplitudes, everyone)
    parts = lax.all_to_all(parts, "mem", 0, 0)
    scale = jnp.exp2(parts[:, rows : rows + 1].astype(jnp.float32) / -FINE)
    ladder = jnp.sum(parts[:, :rows].astype(jnp.float32) * scale, axis=0)
    return (ladder / denominators).astype(jnp.bfloat16)


def solution(mesh):
    return jax.shard_map(
        on_device,
        mesh=mesh,
        in_specs=(
            P("grp", "mem"),
            P("grp", "mem"),
            P("mem", "grp"),
            P("mem", "grp"),
            P("grp", "mem"),
        ),
        out_specs=P("grp", "mem"),
        check_vma=False,
    )
```

```python
import functools

import jax
import jax.numpy as jnp
from jax import lax
from jax.experimental import pallas as pl
from jax.experimental.pallas import tpu as pltpu
from jax.sharding import PartitionSpec as P

NZ = 6
NOTE = 8
LAG = 256.0
FINE = 8.0
VMEM = pl.BlockSpec(memory_space=pltpu.VMEM)
SMEM = pl.BlockSpec(memory_space=pltpu.SMEM)


def to_int16(values):
    return jnp.round(values).astype(jnp.int32).astype(jnp.int16)


def note_of(rows, width):
    at = lax.broadcasted_iota(jnp.int32, (NOTE, width), 0)
    note = jnp.zeros((NOTE, width), jnp.float32)
    for i, row in enumerate(rows):
        note = jnp.where(at == i, row, note)
    return to_int16(note)


def pack_kernel(kt, tile, tiles_ref, integrals_ref, out_ref):
    ones = [tiles_ref[0, k] for k in range(kt)]
    zeros = [sum(1 - ones[j] for j in range(k + 1)) for k in range(kt)]
    notes = []
    for i in range(NZ):
        lag = 0
        for o in range(kt - NZ):
            lag = lag + (zeros[i + o] > o).astype(jnp.int32)
        start = pl.multiple_of((i + lag) * tile, tile)
        block = integrals_ref[pl.ds(start, tile), :].astype(jnp.float32)
        top = jnp.max(jnp.abs(block), axis=0, keepdims=True)
        shift = jnp.floor(14.99 - jnp.log2(jnp.maximum(top, 1e-37)))
        shift = jnp.clip(shift, 0.0, 120.0)
        out_ref[i * tile : (i + 1) * tile] = to_int16(block * jnp.exp2(shift))
        notes.append(shift + LAG * lag.astype(jnp.float32))
    out_ref[NZ * tile :] = note_of(notes, tile)


def ladder_kernel(kt, tile, tiles_ref, amp_ref, packed_ref, out_ref, masked):
    groups = out_ref.shape[0]
    per = packed_ref.shape[0] // groups
    rows = amp_ref.shape[0]

    @pl.when(pl.program_id(0) == 0)
    def _():
        for k in range(kt):
            cols = slice(k * tile, (k + 1) * tile)
            keep = tiles_ref[0, k].astype(jnp.float32)
            masked[:, cols] = (amp_ref[:, cols].astype(jnp.float32) * keep).astype(
                jnp.bfloat16
            )

    for g in range(groups):
        full = []
        for j in range(per):
            b = g * per + j
            note = packed_ref[b, NZ * tile :].astype(jnp.int32).astype(jnp.float32)
            lag = jnp.floor(note / LAG)
            scale = jnp.exp2(LAG * lag - note)
            row = lax.broadcasted_iota(jnp.int32, note.shape, 0)
            scale = jnp.where(row < NZ, scale, 0.0)
            place = jnp.where(lag == 0, scale, 0.0)
            for o in range(1, kt - NZ + 1):
                place = place + pltpu.roll(jnp.where(lag == o, scale, 0.0), o, axis=0)
            place = place.astype(jnp.bfloat16)
            lag = lag.astype(jnp.bfloat16)
            tiles = []
            for i in range(NZ):
                block = packed_ref[b, i * tile : (i + 1) * tile]
                tiles.append(block.astype(jnp.bfloat16))
            for o in range(1, kt - NZ + 1):
                tiles = (
                    tiles[:o]
                    + [
                        jnp.where(lag[i - o : i - o + 1] >= o, tiles[i - 1], tiles[i])
                        for i in range(o, len(tiles))
                    ]
                    + tiles[-1:]
                )
            tiles = [tiles[k] * place[k : k + 1] for k in range(kt)]
            full.append(tiles)
        part = None
        for k in range(0, kt, 2):
            chunk = jnp.concatenate(
                [jnp.concatenate([t[k], t[k + 1]], axis=0) for t in full], axis=1
            )
            term = jnp.dot(
                masked[:, k * tile : (k + 2) * tile],
                chunk,
                preferred_element_type=jnp.float32,
            )
            part = term if part is None else part + term
        top = jnp.max(jnp.abs(part), axis=0, keepdims=True)
        shift = jnp.floor(FINE * (14.999 - jnp.log2(jnp.maximum(top, 1e-37))))
        shift = jnp.minimum(shift, FINE * 125.0)
        out_ref[g, :rows] = to_int16(part * jnp.exp2(shift / FINE))
        out_ref[g, rows:] = note_of([shift], part.shape[1])


def update_kernel(parts_ref, denominators_ref, out_ref):
    rows = denominators_ref.shape[0]
    total = None
    for i in range(parts_ref.shape[0]):
        note = parts_ref[i, rows:].astype(jnp.int32).astype(jnp.float32)
        part = parts_ref[i, :rows].astype(jnp.int32).astype(jnp.float32)
        part = part * jnp.exp2(note[:1] / -FINE)
        total = part if total is None else total + part
    out_ref[...] = (total / denominators_ref[...]).astype(out_ref.dtype)


def on_device(amplitudes, amp_tiles, integrals, int_tiles, denominators):
    rows, depth = amplitudes.shape
    kt = int_tiles.shape[0]
    tile = depth // kt
    owners, width = lax.axis_size("mem"), denominators.shape[1]
    packed = pl.pallas_call(
        functools.partial(pack_kernel, kt, tile),
        out_shape=jax.ShapeDtypeStruct((NZ * tile + NOTE, tile), jnp.int16),
        in_specs=[SMEM, VMEM],
        out_specs=VMEM,
        name="pack",
    )(int_tiles.reshape(1, kt), integrals)
    everyone = lax.all_gather(packed, "grp")
    per = width // tile
    step = 16
    parts = pl.pallas_call(
        functools.partial(ladder_kernel, kt, tile),
        out_shape=jax.ShapeDtypeStruct((owners, rows + NOTE, width), jnp.int16),
        grid=(owners // step,),
        in_specs=[
            SMEM,
            pl.BlockSpec((rows, depth), lambda s: (0, 0)),
            pl.BlockSpec((step * per, NZ * tile + NOTE, tile), lambda s: (s, 0, 0)),
        ],
        out_specs=pl.BlockSpec((step, rows + NOTE, width), lambda s: (s, 0, 0)),
        scratch_shapes=[
            pltpu.VMEM((rows, depth), jnp.bfloat16),
        ],
        compiler_params=pltpu.CompilerParams(vmem_limit_bytes=20 * 2**20),
        name="ladder",
    )(amp_tiles, amplitudes, everyone)
    parts = lax.all_to_all(parts, "mem", 0, 0)
    return pl.pallas_call(
        update_kernel,
        out_shape=jax.ShapeDtypeStruct((rows, width), jnp.bfloat16),
        in_specs=[VMEM, VMEM],
        out_specs=VMEM,
        compiler_params=pltpu.CompilerParams(vmem_limit_bytes=4 * 2**20),
        name="update",
    )(parts, denominators)


def solution(mesh):
    return jax.shard_map(
        on_device,
        mesh=mesh,
        in_specs=(
            P("grp", "mem"),
            P("grp", "mem"),
            P("mem", "grp"),
            P("mem", "grp"),
            P("grp", "mem"),
        ),
        out_specs=P("grp", "mem"),
        check_vma=False,
    )
```

```python
import functools

import jax
import jax.numpy as jnp
from jax import lax
from jax.experimental import pallas as pl
from jax.experimental.pallas import tpu as pltpu
from jax.sharding import PartitionSpec as P

NZ = 6
NOTE = 8
LAG = 256.0
FINE = 8.0
VMEM = pl.BlockSpec(memory_space=pltpu.VMEM)
SMEM = pl.BlockSpec(memory_space=pltpu.SMEM)


def to_int16(values):
    return jnp.round(values).astype(jnp.int32).astype(jnp.int16)


def note_of(rows, width):
    at = lax.broadcasted_iota(jnp.int32, (NOTE, width), 0)
    note = jnp.zeros((NOTE, width), jnp.float32)
    for i, row in enumerate(rows):
        note = jnp.where(at == i, row, note)
    return to_int16(note)


def pack_kernel(kt, tile, tiles_ref, integrals_ref, out_ref):
    ones = [tiles_ref[0, k] for k in range(kt)]
    zeros = [sum(1 - ones[j] for j in range(k + 1)) for k in range(kt)]
    notes = []
    for i in range(NZ):
        lag = 0
        for o in range(kt - NZ):
            lag = lag + (zeros[i + o] > o).astype(jnp.int32)
        start = pl.multiple_of((i + lag) * tile, tile)
        block = integrals_ref[pl.ds(start, tile), :].astype(jnp.float32)
        top = jnp.max(jnp.abs(block), axis=0, keepdims=True)
        shift = jnp.floor(14.99 - jnp.log2(jnp.maximum(top, 1e-37)))
        shift = jnp.clip(shift, 0.0, 120.0)
        out_ref[i * tile : (i + 1) * tile] = to_int16(block * jnp.exp2(shift))
        notes.append(shift + LAG * lag.astype(jnp.float32))
    out_ref[NZ * tile :] = note_of(notes, tile)


def ladder_kernel(kt, tile, tiles_ref, amp_ref, packed_ref, out_ref, masked):
    groups = out_ref.shape[0]
    per = packed_ref.shape[0] // groups
    rows = amp_ref.shape[0]

    @pl.when(pl.program_id(0) == 0)
    def _():
        for k in range(kt):
            cols = slice(k * tile, (k + 1) * tile)
            keep = tiles_ref[0, k].astype(jnp.float32)
            masked[:, cols] = (amp_ref[:, cols].astype(jnp.float32) * keep).astype(
                jnp.bfloat16
            )

    for g in range(groups):
        full = []
        for j in range(per):
            b = g * per + j
            note = packed_ref[b, NZ * tile :].astype(jnp.int32).astype(jnp.float32)
            lag = jnp.floor(note / LAG)
            scale = jnp.exp2(LAG * lag - note)
            row = lax.broadcasted_iota(jnp.int32, note.shape, 0)
            scale = jnp.where(row < NZ, scale, 0.0)
            place = jnp.where(lag == 0, scale, 0.0)
            for o in range(1, kt - NZ + 1):
                place = place + pltpu.roll(jnp.where(lag == o, scale, 0.0), o, axis=0)
            place = place.astype(jnp.bfloat16)
            lag = lag.astype(jnp.bfloat16)
            tiles = []
            for i in range(NZ):
                block = packed_ref[b, i * tile : (i + 1) * tile]
                tiles.append(block.astype(jnp.bfloat16))
            for o in range(1, kt - NZ + 1):
                tiles = (
                    tiles[:o]
                    + [
                        jnp.where(lag[i - o : i - o + 1] >= o, tiles[i - 1], tiles[i])
                        for i in range(o, len(tiles))
                    ]
                    + tiles[-1:]
                )
            tiles = [tiles[k] * place[k : k + 1] for k in range(kt)]
            full.append(tiles)
        whole = jnp.concatenate([jnp.concatenate(t, axis=0) for t in full], axis=1)
        part = jnp.dot(masked[...], whole, preferred_element_type=jnp.float32)
        top = jnp.max(jnp.abs(part), axis=0, keepdims=True)
        shift = jnp.floor(FINE * (14.999 - jnp.log2(jnp.maximum(top, 1e-37))))
        shift = jnp.minimum(shift, FINE * 125.0)
        out_ref[g, :rows] = to_int16(part * jnp.exp2(shift / FINE))
        out_ref[g, rows:] = note_of([shift], part.shape[1])


def update_kernel(parts_ref, denominators_ref, out_ref):
    rows = denominators_ref.shape[0]
    total = None
    for i in range(parts_ref.shape[0]):
        note = parts_ref[i, rows:].astype(jnp.int32).astype(jnp.float32)
        part = parts_ref[i, :rows].astype(jnp.int32).astype(jnp.float32)
        part = part * jnp.exp2(note[:1] / -FINE)
        total = part if total is None else total + part
    out_ref[...] = (total / denominators_ref[...]).astype(out_ref.dtype)


def on_device(amplitudes, amp_tiles, integrals, int_tiles, denominators):
    rows, depth = amplitudes.shape
    kt = int_tiles.shape[0]
    tile = depth // kt
    owners, width = lax.axis_size("mem"), denominators.shape[1]
    packed = pl.pallas_call(
        functools.partial(pack_kernel, kt, tile),
        out_shape=jax.ShapeDtypeStruct((NZ * tile + NOTE, tile), jnp.int16),
        in_specs=[SMEM, VMEM],
        out_specs=VMEM,
        name="pack",
    )(int_tiles.reshape(1, kt), integrals)
    everyone = lax.all_gather(packed, "grp")
    per = width // tile
    step = 16
    parts = pl.pallas_call(
        functools.partial(ladder_kernel, kt, tile),
        out_shape=jax.ShapeDtypeStruct((owners, rows + NOTE, width), jnp.int16),
        grid=(owners // step,),
        in_specs=[
            SMEM,
            pl.BlockSpec((rows, depth), lambda s: (0, 0)),
            pl.BlockSpec((step * per, NZ * tile + NOTE, tile), lambda s: (s, 0, 0)),
        ],
        out_specs=pl.BlockSpec((step, rows + NOTE, width), lambda s: (s, 0, 0)),
        scratch_shapes=[
            pltpu.VMEM((rows, depth), jnp.bfloat16),
        ],
        compiler_params=pltpu.CompilerParams(vmem_limit_bytes=20 * 2**20),
        name="ladder",
    )(amp_tiles, amplitudes, everyone)
    parts = lax.all_to_all(parts, "mem", 0, 0)
    return pl.pallas_call(
        update_kernel,
        out_shape=jax.ShapeDtypeStruct((rows, width), jnp.bfloat16),
        in_specs=[VMEM, VMEM],
        out_specs=VMEM,
        compiler_params=pltpu.CompilerParams(vmem_limit_bytes=4 * 2**20),
        name="update",
    )(parts, denominators)


def solution(mesh):
    return jax.shard_map(
        on_device,
        mesh=mesh,
        in_specs=(
            P("grp", "mem"),
            P("grp", "mem"),
            P("mem", "grp"),
            P("mem", "grp"),
            P("grp", "mem"),
        ),
        out_specs=P("grp", "mem"),
        check_vma=False,
    )
```

```python
import functools

import jax
import jax.numpy as jnp
from jax import lax
from jax.experimental import pallas as pl
from jax.experimental.pallas import tpu as pltpu
from jax.sharding import PartitionSpec as P

NZ = 6
NOTE = 8
LAG = 256.0
FINE = 8.0
VMEM = pl.BlockSpec(memory_space=pltpu.VMEM)
SMEM = pl.BlockSpec(memory_space=pltpu.SMEM)


def to_int16(values):
    return jnp.round(values).astype(jnp.int32).astype(jnp.int16)


def note_of(rows, width):
    at = lax.broadcasted_iota(jnp.int32, (NOTE, width), 0)
    note = jnp.zeros((NOTE, width), jnp.float32)
    for i, row in enumerate(rows):
        note = jnp.where(at == i, row, note)
    return to_int16(note)


def pack_kernel(kt, tile, tiles_ref, integrals_ref, out_ref):
    ones = [
        jnp.broadcast_to(tiles_ref[:, k : k + 1].astype(jnp.float32), (1, tile))
        for k in range(kt)
    ]
    zeros = [sum(1.0 - ones[j] for j in range(k + 1)) for k in range(kt)]
    notes = []
    for i in range(NZ):
        block = integrals_ref[(kt - NZ + i) * tile : (kt - NZ + i + 1) * tile]
        block = block.astype(jnp.float32)
        lag = jnp.zeros((1, tile), jnp.float32)
        for o in range(kt - NZ - 1, -1, -1):
            nearer = integrals_ref[(i + o) * tile : (i + o + 1) * tile]
            block = jnp.where(zeros[i + o] > o, block, nearer.astype(jnp.float32))
            lag = lag + jnp.where(zeros[i + o] > o, 1.0, 0.0)
        top = jnp.max(jnp.abs(block), axis=0, keepdims=True)
        shift = jnp.floor(14.99 - jnp.log2(jnp.maximum(top, 1e-37)))
        shift = jnp.clip(shift, 0.0, 120.0)
        out_ref[i * tile : (i + 1) * tile] = to_int16(block * jnp.exp2(shift))
        notes.append(shift + LAG * lag)
    out_ref[NZ * tile :] = note_of(notes, tile)


def ladder_kernel(kt, tile, tiles_ref, amp_ref, packed_ref, out_ref, masked):
    groups = out_ref.shape[0]
    per = packed_ref.shape[0] // groups
    rows = amp_ref.shape[0]

    @pl.when(pl.program_id(0) == 0)
    def _():
        for k in range(kt):
            cols = slice(k * tile, (k + 1) * tile)
            keep = tiles_ref[0, k].astype(jnp.float32)
            masked[:, cols] = (amp_ref[:, cols].astype(jnp.float32) * keep).astype(
                jnp.bfloat16
            )

    for g in range(groups):
        full = []
        for j in range(per):
            b = g * per + j
            note = packed_ref[b, NZ * tile :].astype(jnp.int32).astype(jnp.float32)
            lag = jnp.floor(note / LAG)
            scale = jnp.exp2(LAG * lag - note)
            row = lax.broadcasted_iota(jnp.int32, note.shape, 0)
            scale = jnp.where(row < NZ, scale, 0.0)
            place = jnp.where(lag == 0, scale, 0.0)
            for o in range(1, kt - NZ + 1):
                place = place + pltpu.roll(jnp.where(lag == o, scale, 0.0), o, axis=0)
            place = place.astype(jnp.bfloat16)
            lag = lag.astype(jnp.bfloat16)
            tiles = []
            for i in range(NZ):
                block = packed_ref[b, i * tile : (i + 1) * tile]
                tiles.append(block.astype(jnp.bfloat16))
            for o in range(1, kt - NZ + 1):
                tiles = (
                    tiles[:o]
                    + [
                        jnp.where(lag[i - o : i - o + 1] >= o, tiles[i - 1], tiles[i])
                        for i in range(o, len(tiles))
                    ]
                    + tiles[-1:]
                )
            tiles = [tiles[k] * place[k : k + 1] for k in range(kt)]
            full.append(tiles)
        part = None
        for k in range(0, kt, 2):
            chunk = jnp.concatenate(
                [jnp.concatenate([t[k], t[k + 1]], axis=0) for t in full], axis=1
            )
            term = jnp.dot(
                masked[:, k * tile : (k + 2) * tile],
                chunk,
                preferred_element_type=jnp.float32,
            )
            part = term if part is None else part + term
        top = jnp.max(jnp.abs(part), axis=0, keepdims=True)
        shift = jnp.floor(FINE * (14.999 - jnp.log2(jnp.maximum(top, 1e-37))))
        shift = jnp.minimum(shift, FINE * 125.0)
        out_ref[g, :rows] = to_int16(part * jnp.exp2(shift / FINE))
        out_ref[g, rows:] = note_of([shift], part.shape[1])


def update_kernel(parts_ref, denominators_ref, out_ref):
    rows = denominators_ref.shape[0]
    total = None
    for i in range(parts_ref.shape[0]):
        note = parts_ref[i, rows:].astype(jnp.int32).astype(jnp.float32)
        part = parts_ref[i, :rows].astype(jnp.int32).astype(jnp.float32)
        part = part * jnp.exp2(note[:1] / -FINE)
        total = part if total is None else total + part
    out_ref[...] = (total / denominators_ref[...]).astype(out_ref.dtype)


def on_device(amplitudes, amp_tiles, integrals, int_tiles, denominators):
    rows, depth = amplitudes.shape
    kt = int_tiles.shape[0]
    tile = depth // kt
    owners, width = lax.axis_size("mem"), denominators.shape[1]
    packed = pl.pallas_call(
        functools.partial(pack_kernel, kt, tile),
        out_shape=jax.ShapeDtypeStruct((NZ * tile + NOTE, tile), jnp.int16),
        in_specs=[VMEM, VMEM],
        out_specs=VMEM,
        name="pack",
    )(int_tiles.reshape(1, kt), integrals)
    everyone = lax.all_gather(packed, "grp")
    per = width // tile
    step = 16
    parts = pl.pallas_call(
        functools.partial(ladder_kernel, kt, tile),
        out_shape=jax.ShapeDtypeStruct((owners, rows + NOTE, width), jnp.int16),
        grid=(owners // step,),
        in_specs=[
            SMEM,
            pl.BlockSpec((rows, depth), lambda s: (0, 0)),
            pl.BlockSpec((step * per, NZ * tile + NOTE, tile), lambda s: (s, 0, 0)),
        ],
        out_specs=pl.BlockSpec((step, rows + NOTE, width), lambda s: (s, 0, 0)),
        scratch_shapes=[
            pltpu.VMEM((rows, depth), jnp.bfloat16),
        ],
        compiler_params=pltpu.CompilerParams(vmem_limit_bytes=20 * 2**20),
        name="ladder",
    )(amp_tiles, amplitudes, everyone)
    parts = lax.all_to_all(parts, "mem", 0, 0)
    return pl.pallas_call(
        update_kernel,
        out_shape=jax.ShapeDtypeStruct((rows, width), jnp.bfloat16),
        in_specs=[VMEM, VMEM],
        out_specs=VMEM,
        compiler_params=pltpu.CompilerParams(vmem_limit_bytes=4 * 2**20),
        name="update",
    )(parts, denominators)


def solution(mesh):
    return jax.shard_map(
        on_device,
        mesh=mesh,
        in_specs=(
            P("grp", "mem"),
            P("grp", "mem"),
            P("mem", "grp"),
            P("mem", "grp"),
            P("grp", "mem"),
        ),
        out_specs=P("grp", "mem"),
        check_vma=False,
    )
```
